32 devices in a mesh: ctx: 8 (over y, x, core), mp: 4 (over z).
Axes of the slice: x: 2, y: 2, z: 4, core: 2. Of those that a mesh axis runs over, the one named last changes fastest.
Arguments:
- source_rows: bfloat16 [4096, 3, 8192], P('ctx', None, 'mp'), may hold values from -6 to 6
- short_filters: bfloat16 [3, 7, 8192], P(None, None, 'mp'), may hold values from -2 to 2
- medium_filters: bfloat16 [128, 512], P(None, 'mp'), may hold values from -0.5 to 0.5
- skip_gain: float32 [8192], P('mp'), may hold values from 0.1 to 1.9
- out_weight: bfloat16 [8192, 8192], P('mp', 'ctx'), may hold values from -0.0625 to 0.0625
- doc_lengths: int32 [8], replicated, may hold values from 1 to 512, 2048 in all
- block_packing_device: int32 [8, 4], replicated, may hold values from 0 to 7, as said below
Outputs:
- mixed: bfloat16 [2048, 8192], P('ctx', 'mp')
The draws below stay inside these ranges and needn't reach their ends.
Inputs may be any that keep to these rules, and one draw needn't show every extreme that they name: `block_packing_device`: row c names, for the 4 blocks of stretch c in order, the packing device that holds each; the entries of one row differ, and some packing device is named in every row. A packing device keeps the blocks it holds in increasing order of their stretch, in its first slots.
All inputs are finite; a program needn't handle non-finite values.
Results may differ from the reference program's by a relative error of at most 0.02.
Values may be sent and summed in bfloat16 or wider, within the bound.
A program may use at most 192 MiB of HBM per device.

```python
import math
import jax
import jax.numpy as jnp
import numpy as np
from jax import lax

D = 8192
GROUPS = 512
SE_LEN = 7
MR_LEN = 128
DOCS = 8
STRETCHES = 8
NB_OWN = 4
BLK = 64
SRC_ROWS = 512
TOKENS = 2048
WIDTH_DEV = 2048
DOC_MOST = 512


def draw_block_packing_device(key, part):
    base = jax.random.fold_in(key, 11)
    key_heavy, key_bias, key_score = jax.random.split(base, 3)
    heavy_blocks = jax.random.randint(key_heavy, (), 0, STRETCHES)
    level_values = jax.random.randint(key_bias, (STRETCHES,), 0, 4)
    random_noise = jax.random.randint(key_score, (STRETCHES, STRETCHES), 0, 4096)
    block_owners = jnp.arange(STRETCHES, dtype=jnp.int32)
    extra_reward = jnp.where(block_owners == heavy_blocks, 100000, 0).astype(jnp.int32)
    block_score = random_noise + level_values[None, :] * 1024 + extra_reward[None, :]
    block_score = block_score * STRETCHES + block_owners[None, :]
    picked = lax.top_k(block_score, NB_OWN)[1]
    return picked.astype(jnp.int32)


def level_of(rng, extent, pieces, smallest, top_value):
    def one(dim, blocks):
        heights = jax.random.uniform(jax.random.fold_in(jax.random.fold_in(rng, 6), dim), (blocks,), jnp.float32, smallest / len(pieces), top_value / len(pieces))
        return jnp.repeat(jnp.exp(heights), extent[dim] // blocks).reshape((-1,) + (1,) * (len(extent) - dim - 1))

    gain = one(*pieces[0])
    for cut in pieces[1:]:
        gain = gain * one(*cut)
    return gain


def profile(count, total, bound, lean):
    loads = [(1 << 20) // math.isqrt(standing ** lean) + 1 for standing in range(2, count + 1)]
    rest, counts = total - bound - (count - 1), [1] * (count - 1)
    while rest > 0:
        candidates = [i for i in range(count - 1) if counts[i] < bound]
        whole, remaining = sum([loads[i] for i in candidates]), rest
        for i in candidates:
            addition = min(bound - counts[i], max(1, remaining * loads[i] // whole), rest)
            counts[i] = counts[i] + addition
            rest = rest - addition
    return np.array([bound] + counts)


def ragged_sizes(own_key, amount, total, limit, slope):
    if amount == 2:
        one = jax.random.randint(own_key, (), max(1, total - limit), min(limit, total - 1) + 1)
        return jnp.stack([one, total - one])
    lengths = jnp.asarray(profile(amount, total, limit, slope), jnp.int32)
    couples = (amount - 1) // 2
    source_of, receiver = lengths[1:1 + 2 * couples:2], lengths[2:2 + 2 * couples:2]
    room = jnp.minimum(source_of - 1, limit - receiver)
    moved = jax.random.randint(jax.random.fold_in(own_key, 1), (couples,), 0, 1 << 20) % (room + 1)
    lengths = lengths.at[1:1 + 2 * couples:2].set(source_of - moved).at[2:2 + 2 * couples:2].set(receiver + moved)
    return lengths[jax.random.permutation(jax.random.fold_in(own_key, 2), amount)]


def noise(rng, dims, width, limit, shards=(), held_as=jnp.bfloat16):
    array = width * jax.random.normal(rng, dims, jnp.float32)
    if shards:
        array = array * level_of(rng, dims, shards, -0.22, 0.18)
    return jnp.clip(array, -limit, limit).astype(held_as)


def setup_inputs(seed: int = 0) -> dict:
    keys = jax.random.split(jax.random.key(seed), 8)
    source_rows = noise(keys[0], (STRETCHES * SRC_ROWS, 3, D), 1.0, 6.0, ((0, 8), (2, 4)))
    short_filters = noise(keys[1], (3, SE_LEN, D), SE_LEN ** -0.5, 2.0, ((2, 4),))
    medium_filters = noise(keys[2], (MR_LEN, GROUPS), MR_LEN ** -0.5, 0.5, ((1, 4),))
    skip_gain = jnp.clip(1.0 + 0.18 * jax.random.normal(keys[3], (D,), jnp.float32), 0.1, 1.9)
    out_weight = noise(keys[4], (D, D), D ** -0.5, 0.0625, ((0, 4), (1, 8)))
    doc_lengths = ragged_sizes(keys[5], DOCS, TOKENS, DOC_MOST, 2).astype(jnp.int32)
    block_packing_device = draw_block_packing_device(jax.random.fold_in(keys[7], 71), 0)
    return {"source_rows": source_rows, "short_filters": short_filters, "medium_filters": medium_filters, "skip_gain": skip_gain, "out_weight": out_weight, "doc_lengths": doc_lengths, "block_packing_device": block_packing_device}


def short_conv(data, filt, back):
    rows = data.shape[0]
    padded = jnp.pad(data.astype(jnp.float32), ((SE_LEN - 1, 0), (0, 0)))
    taps = filt.astype(jnp.float32)
    total = jnp.zeros((rows, data.shape[1]), jnp.float32)
    for step in range(SE_LEN):
        keep = (back >= step).astype(jnp.float32)[:, None]
        piece = padded[SE_LEN - 1 - step:SE_LEN - 1 - step + rows]
        total = total + taps[step][None, :] * piece * keep
    return total


def reference(source_rows, short_filters, medium_filters, skip_gain, out_weight, doc_lengths, block_packing_device):
    ends = jnp.cumsum(doc_lengths).astype(jnp.int32)
    starts = (ends - doc_lengths).astype(jnp.int32)
    where_row = jnp.arange(TOKENS, dtype=jnp.int32)
    begin = jnp.max(jnp.where(starts[None, :] <= where_row[:, None], starts[None, :], 0), axis=1).astype(jnp.int32)
    back = (where_row - begin).astype(jnp.int32)
    block_owners = jnp.arange(STRETCHES, dtype=jnp.int32)
    member = jnp.any(block_packing_device[:, :, None] == block_owners[None, None, :], axis=1).astype(jnp.int32)
    before = (jnp.cumsum(member, axis=0) - member).astype(jnp.int32)
    ranks = jnp.take_along_axis(before, block_packing_device, axis=1).astype(jnp.int32)
    first = (block_packing_device * SRC_ROWS + ranks * BLK).reshape(-1).astype(jnp.int32)
    index_rows = (first[:, None] + jnp.arange(BLK, dtype=jnp.int32)[None, :]).reshape(-1).astype(jnp.int32)
    packed = jnp.take(source_rows, index_rows, axis=0)
    query = short_conv(packed[:, 0], short_filters[0], back)
    keyed = short_conv(packed[:, 1], short_filters[1], back)
    valued = short_conv(packed[:, 2], short_filters[2], back)
    z_vals = (keyed * valued).astype(jnp.bfloat16)
    z_wide = z_vals.astype(jnp.float32)
    zpad = jnp.pad(z_wide, ((MR_LEN - 1, 0), (0, 0)))
    taps = jnp.repeat(medium_filters.astype(jnp.float32), D // GROUPS, axis=1)

    def add_tap(step, total):
        step = jnp.asarray(step).astype(jnp.int32)
        offset = (MR_LEN - 1 - step).astype(jnp.int32)
        piece = lax.dynamic_slice_in_dim(zpad, offset, TOKENS, 0)
        tap = lax.dynamic_slice_in_dim(taps, step, 1, 0)
        keep = (back >= step).astype(jnp.float32)[:, None]
        return total + tap * piece * keep

    medium = lax.fori_loop(0, MR_LEN, add_tap, jnp.zeros((TOKENS, D), jnp.float32))
    hidden = (query * (medium + skip_gain[None, :] * z_wide)).astype(jnp.bfloat16)
    mixed = jnp.zeros((TOKENS, D), jnp.float32)
    for block in range(D // WIDTH_DEV):
        lo = block * WIDTH_DEV
        part = jnp.dot(hidden[:, lo:lo + WIDTH_DEV], out_weight[lo:lo + WIDTH_DEV], preferred_element_type=jnp.float32)
        part = lax.optimization_barrier(part.astype(jnp.bfloat16))
        mixed = mixed + part.astype(jnp.float32)
    return mixed.astype(jnp.bfloat16)
```

```python
import functools

import jax
import jax.numpy as jnp
from jax import lax
from jax.experimental import pallas as pl
from jax.experimental.pallas import tpu as pltpu
from jax.sharding import PartitionSpec as P

MESH = pl.DeviceIdType.MESH
EDGE = 16


def flipped(index, distance):
    bit = 1
    while bit <= distance:
        if distance & bit:
            index = index + bit * (1 - 2 * (lax.div(index, bit) % 2))
        bit *= 2
    return index


def passed_along(block, axis, distance):
    devices = range(lax.axis_size(axis))
    route = [(i - distance, i) for i in devices if i - distance in devices]
    return lax.ppermute(block, axis, route)


def exchange_kernel(n, out_ref, in_ref, send_sem, recv_sem, own_sem):
    me = lax.axis_index("ctx")
    mp = lax.axis_index("mp")
    barrier = pltpu.get_barrier_semaphore()
    for d in range(1, n):
        pl.semaphore_signal(barrier, inc=1, device_id=(flipped(me, d), mp), device_id_type=MESH)
    pl.semaphore_wait(barrier, n - 1)
    copies = []
    for d in reversed(range(1, n)):
        peer = flipped(me, d)
        copy = pltpu.make_async_remote_copy(
            src_ref=out_ref.at[peer],
            dst_ref=in_ref.at[me],
            send_sem=send_sem.at[d],
            recv_sem=recv_sem.at[d],
            device_id=(peer, mp),
            device_id_type=MESH,
        )
        copy.start()
        copies.append(copy)
    own = pltpu.make_async_copy(out_ref.at[me], in_ref.at[me], own_sem)
    own.start()
    own.wait()
    for d in range(1, n):
        peer = flipped(me, d)
        pltpu.make_async_remote_copy(
            src_ref=out_ref.at[peer],
            dst_ref=in_ref.at[peer],
            send_sem=send_sem.at[d],
            recv_sem=recv_sem.at[d],
            device_id=(peer, mp),
            device_id_type=MESH,
        ).wait()


def exchange(outgoing):
    n = outgoing.shape[0]
    return pl.pallas_call(
        functools.partial(exchange_kernel, n),
        out_shape=jax.ShapeDtypeStruct(outgoing.shape, outgoing.dtype),
        in_specs=[pl.BlockSpec(memory_space=pl.ANY)],
        out_specs=pl.BlockSpec(memory_space=pl.ANY),
        scratch_shapes=[
            pltpu.SemaphoreType.DMA((n,)),
            pltpu.SemaphoreType.DMA((n,)),
            pltpu.SemaphoreType.DMA,
        ],
        compiler_params=pltpu.CompilerParams(collective_id=0, has_side_effects=True),
        name="exchange",
    )(outgoing)


def short_kernel(nb, wanted_ref, *refs):
    block_refs = refs[:nb]
    edge_ref, filt_ref, back_ref, q_ref, z_ref = refs[nb:]
    back = back_ref[...]
    rows, lanes = q_ref.shape
    span = filt_ref.shape[1]

    def conv(i, sl):
        ext = jnp.concatenate(
            [edge_ref[i, :, sl].astype(jnp.float32)]
            + [b[0, i, :, sl].astype(jnp.float32) for b in block_refs],
            axis=0,
        )
        total = filt_ref[i, 0:1, sl] * ext[EDGE:]
        for j in range(1, span):
            piece = ext[EDGE - j : EDGE - j + rows]
            total = total + filt_ref[i, j : j + 1, sl] * jnp.where(back >= j, piece, 0.0)
        return total

    for lo in range(0, lanes, 128):
        sl = slice(lo, lo + 128)
        q_ref[:, sl] = conv(0, sl)
        z_ref[:, sl] = (conv(1, sl) * conv(2, sl)).astype(z_ref.dtype)


def short_stage(incoming, wanted, edge, filt, back):
    n, _, blk, width = incoming.shape
    nb = wanted.shape[0]
    rows = nb * blk
    lanes = 256
    in_specs = [
        pl.BlockSpec((1, 3, blk, lanes), functools.partial(lambda k, i, w: (w[k], 0, 0, i), k))
        for k in range(nb)
    ] + [
        pl.BlockSpec((3, EDGE, lanes), lambda i, w: (0, 0, i)),
        pl.BlockSpec((3, filt.shape[1], lanes), lambda i, w: (0, 0, i)),
        pl.BlockSpec((rows, 128), lambda i, w: (0, 0)),
    ]
    return pl.pallas_call(
        functools.partial(short_kernel, nb),
        grid_spec=pltpu.PrefetchScalarGridSpec(
            num_scalar_prefetch=1,
            grid=(width // lanes,),
            in_specs=in_specs,
            out_specs=[
                pl.BlockSpec((rows, lanes), lambda i, w: (0, i)),
                pl.BlockSpec((rows, lanes), lambda i, w: (0, i)),
            ],
        ),
        out_shape=[
            jax.ShapeDtypeStruct((rows, width), jnp.float32),
            jax.ShapeDtypeStruct((rows, width), jnp.bfloat16),
        ],
        compiler_params=pltpu.CompilerParams(vmem_limit_bytes=48 * 2**20),
        name="short_conv",
    )(wanted, *([incoming] * nb), edge, filt, back)


def medium_kernel(per_group, span, prev_ref, z_ref, q_ref, skip_ref, line_ref, back_ref, h_ref):
    rows, lanes = z_ref.shape
    row = lax.broadcasted_iota(jnp.int32, (span, 2 * span), 0)
    col = lax.broadcasted_iota(jnp.int32, (span, 2 * span), 1)
    step = span + row - col
    lane = lax.broadcasted_iota(jnp.int32, (span, 128), 1)
    tiles = rows // span
    keeps = [
        step <= jnp.concatenate([back_ref[r * span : (r + 1) * span]] * 2, axis=1)
        for r in range(tiles)
    ]
    groups = 128 // per_group
    for lo in range(0, lanes, 128):
        sl = slice(lo, lo + 128)
        ext = jnp.concatenate([prev_ref[:, sl], z_ref[:, sl]], axis=0)
        total = [jnp.zeros((span, 128), jnp.float32) for _ in range(tiles)]
        for g in range(groups):
            line = line_ref[0, lo // per_group + g : lo // per_group + g + 1, :]
            band = pltpu.roll(
                jnp.broadcast_to(line, (span, 2 * span)), 0, 1, stride=1, stride_axis=0
            )
            mine = (lane >= g * per_group) & (lane < (g + 1) * per_group)
            for r in range(tiles):
                kept = jnp.where(keeps[r], band, 0.0).astype(jnp.bfloat16)
                part = jnp.dot(
                    kept,
                    ext[r * span : (r + 2) * span],
                    preferred_element_type=jnp.float32,
                )
                total[r] = jnp.where(mine, part, total[r])
        for r in range(tiles):
            rs = slice(r * span, (r + 1) * span)
            full = total[r] + skip_ref[0:1, sl] * z_ref[rs, sl].astype(jnp.float32)
            h_ref[rs, sl] = (q_ref[rs, sl] * full).astype(h_ref.dtype)


def medium_stage(z_prev, z_vals, query, skip, taps, back):
    rows, width = z_vals.shape
    span, groups = taps.shape
    per_group = width // groups
    lanes = 256
    line = jnp.concatenate(
        [
            jnp.zeros((groups, 1), jnp.float32),
            jnp.transpose(taps[::-1]).astype(jnp.float32),
            jnp.zeros((groups, span - 1), jnp.float32),
        ],
        axis=1,
    ).reshape(width // lanes, lanes // per_group, 2 * span)
    return pl.pallas_call(
        functools.partial(medium_kernel, per_group, span),
        grid=(width // lanes,),
        in_specs=[
            pl.BlockSpec((span, lanes), lambda i: (0, i)),
            pl.BlockSpec((rows, lanes), lambda i: (0, i)),
            pl.BlockSpec((rows, lanes), lambda i: (0, i)),
            pl.BlockSpec((1, lanes), lambda i: (0, i)),
            pl.BlockSpec((1, lanes // per_group, 2 * span), lambda i: (i, 0, 0)),
            pl.BlockSpec((rows, 128), lambda i: (0, 0)),
        ],
        out_specs=pl.BlockSpec((rows, lanes), lambda i: (0, i)),
        out_shape=jax.ShapeDtypeStruct((rows, width), jnp.bfloat16),
        compiler_params=pltpu.CompilerParams(vmem_limit_bytes=48 * 2**20),
        name="medium_conv",
    )(z_prev, z_vals, query, skip, line, back)


def project_kernel(
    n, m, hid_ref, w_ref, out_ref, hid, pout, pin, zin,
    own_sem, hsend, hrecv, psend, precv, zsend, zrecv,
):
    c = lax.axis_index("ctx")
    z = lax.axis_index("mp")
    share = n // m
    rows = hid_ref.shape[0]
    cols = w_ref.shape[1]

    barrier = pltpu.get_barrier_semaphore()
    for d in range(1, n):
        pl.semaphore_signal(barrier, inc=1, device_id=(flipped(c, d), z), device_id_type=MESH)
    for s in range(1, m):
        pl.semaphore_signal(barrier, inc=1, device_id=(c, flipped(z, s)), device_id_type=MESH)
    pl.semaphore_wait(barrier, n - 1 + m - 1)

    sent = []

    def send_hidden(origin, peer, slot, src):
        copy = pltpu.make_async_remote_copy(
            src_ref=src,
            dst_ref=hid.at[origin],
            send_sem=hsend.at[slot],
            recv_sem=hrecv.at[origin],
            device_id=(peer, z),
            device_id_type=MESH,
        )
        copy.start()
        sent.append(copy)

    def hidden_arrived(origin):
        pltpu.make_async_remote_copy(
            src_ref=hid_ref,
            dst_ref=hid.at[origin],
            send_sem=hsend.at[0],
            recv_sem=hrecv.at[origin],
            device_id=(flipped(c, 1), z),
            device_id_type=MESH,
        ).wait_recv()

    def multiply(origin, d, src):
        @pl.loop(0, cols // 256)
        def _(i):
            at = pl.ds(pl.multiple_of(i * 256, 256), 256)
            pout[d, :, at] = jnp.dot(
                src[...], w_ref[:, at], preferred_element_type=jnp.float32
            ).astype(jnp.bfloat16)

        if d == 0:
            copy = pltpu.make_async_copy(pout.at[0], pin.at[c], precv.at[c])
        else:
            copy = pltpu.make_async_remote_copy(
                src_ref=pout.at[d],
                dst_ref=pin.at[c],
                send_sem=psend.at[d],
                recv_sem=precv.at[c],
                device_id=(origin, z),
                device_id_type=MESH,
            )
            sent.append(copy)
        copy.start()

    mate = flipped(c, 1)
    if n == 8:
        core = c % 2
        x_peer, y_peer = flipped(c, 2), flipped(c, 4)
        first = x_peer + (y_peer - x_peer) * core
        second = y_peer + (x_peer - y_peer) * core
        across = flipped(c, 6)
        send_hidden(c, first, 1, hid_ref)
        send_hidden(c, second, 2, hid_ref)
        send_hidden(c, mate, 3, hid_ref)
        multiply(c, 0, hid_ref)
        hidden_arrived(first)
        send_hidden(first, second, 4, hid.at[first])
        send_hidden(first, mate, 5, hid.at[first])
        hidden_arrived(second)
        send_hidden(second, mate, 6, hid.at[second])
        hidden_arrived(mate)
        multiply(mate, 1, hid.at[mate])
        multiply(first, 2, hid.at[first])
        multiply(second, 4, hid.at[second])
        hidden_arrived(flipped(second, 1))
        multiply(flipped(second, 1), 5, hid.at[flipped(second, 1)])
        hidden_arrived(flipped(first, 1))
        multiply(flipped(first, 1), 3, hid.at[flipped(first, 1)])
        hidden_arrived(across)
        send_hidden(across, mate, 7, hid.at[across])
        multiply(across, 6, hid.at[across])
        hidden_arrived(flipped(across, 1))
        multiply(flipped(across, 1), 7, hid.at[flipped(across, 1)])
    else:
        for d in range(1, n):
            send_hidden(c, flipped(c, d), d, hid_ref)
        multiply(c, 0, hid_ref)
        for d in range(1, n):
            origin = flipped(c, d)
            hidden_arrived(origin)
            multiply(origin, d, hid.at[origin])

    home = lax.div(c, share)

    def forward(plane, t, h):
        return pltpu.make_async_remote_copy(
            src_ref=pin.at[plane * share + h],
            dst_ref=zin.at[z, h],
            send_sem=zsend.at[t, h],
            recv_sem=zrecv.at[z, h],
            device_id=(c, plane),
            device_id_type=MESH,
        )

    for t in range(m):
        plane = flipped(home, t)
        for h in range(share):
            block = plane * share + h
            pltpu.make_async_copy(pout.at[0], pin.at[block], precv.at[block]).wait()

            @pl.when(plane != z)
            def _(plane=plane, t=t, h=h):
                forward(plane, t, h).start()

    for s in range(1, m):
        other = flipped(z, s)
        for h in range(share):
            pltpu.make_async_remote_copy(
                src_ref=pin.at[0],
                dst_ref=zin.at[other, h],
                send_sem=zsend.at[0, 0],
                recv_sem=zrecv.at[other, h],
                device_id=(c, other),
                device_id_type=MESH,
            ).wait_recv()
    for h in range(share):
        total = pin[z * share + h].astype(jnp.float32)
        for s in range(1, m):
            total = total + zin[flipped(z, s), h].astype(jnp.float32)
        out_ref[:, h * cols : (h + 1) * cols] = total.astype(out_ref.dtype)

    for copy in sent:
        copy.wait_send()
    for t in range(m):
        plane = flipped(home, t)
        for h in range(share):

            @pl.when(plane != z)
            def _(plane=plane, t=t, h=h):
                forward(plane, t, h).wait_send()


def project(hidden, weight):
    n, m = lax.axis_size("ctx"), lax.axis_size("mp")
    share = n // m
    rows, depth = hidden.shape
    cols = weight.shape[1]
    bf16 = jnp.bfloat16
    dma = pltpu.SemaphoreType.DMA
    return pl.pallas_call(
        functools.partial(project_kernel, n, m),
        out_shape=jax.ShapeDtypeStruct((rows, share * cols), bf16),
        in_specs=[pl.BlockSpec(memory_space=pltpu.VMEM)] * 2,
        out_specs=pl.BlockSpec(memory_space=pltpu.VMEM),
        scratch_shapes=[
            pltpu.VMEM((n, rows, depth), bf16),
            pltpu.VMEM((n, rows, cols), bf16),
            pltpu.VMEM((n, rows, cols), bf16),
            pltpu.VMEM((m, share, rows, cols), bf16),
            dma,
            dma((n,)),
            dma((n,)),
            dma((n,)),
            dma((n,)),
            dma((m, share)),
            dma((m, share)),
        ],
        compiler_params=pltpu.CompilerParams(
            collective_id=1, has_side_effects=True, vmem_limit_bytes=50 * 2**20
        ),
        name="project",
    )(hidden, weight)


def on_device(
    source_rows,
    short_filters,
    medium_filters,
    skip_gain,
    out_weight,
    doc_lengths,
    block_packing_device,
):
    stretches = lax.axis_size("ctx")
    me = lax.axis_index("ctx")
    nb_own = block_packing_device.shape[1]
    blk = source_rows.shape[0] // stretches
    rows = nb_own * blk
    width = source_rows.shape[2]
    mr_len = medium_filters.shape[0]
    member = jnp.any(block_packing_device == me, axis=1)
    flags = member.astype(jnp.int32)
    slots = jnp.minimum(jnp.cumsum(flags) - flags, stretches - 1)
    blocks = source_rows.reshape(stretches, blk, 3, width)
    outgoing = jnp.take(blocks, slots, axis=0, mode="clip").transpose(0, 2, 1, 3)
    incoming = exchange(outgoing)
    wanted = lax.dynamic_index_in_dim(block_packing_device, me, 0, keepdims=False)

    ends = jnp.cumsum(doc_lengths)
    starts = ends - doc_lengths
    positions = me * rows + jnp.arange(rows, dtype=jnp.int32)
    begin = jnp.max(jnp.where(starts[None, :] <= positions[:, None], starts[None, :], 0), axis=1)
    back = jnp.broadcast_to((positions - begin)[:, None], (rows, 128))

    last = lax.dynamic_index_in_dim(incoming, wanted[nb_own - 1], 0, keepdims=False)
    edge = passed_along(last[:, blk - EDGE :], "ctx", 1)
    query, z_vals = short_stage(incoming, wanted, edge, short_filters.astype(jnp.float32), back)
    z_prev = passed_along(z_vals[rows - mr_len :], "ctx", 1)
    hidden = medium_stage(z_prev, z_vals, query, skip_gain[None, :], medium_filters, back)
    return project(hidden, out_weight)


def solution(mesh):
    return jax.shard_map(
        on_device,
        mesh=mesh,
        in_specs=(
            P("ctx", None, "mp"),
            P(None, None, "mp"),
            P(None, "mp"),
            P("mp"),
            P("mp", "ctx"),
            P(),
            P(),
        ),
        out_specs=P("ctx", "mp"),
        check_vma=False,
    )
```

```python
import functools

import jax
import jax.numpy as jnp
from jax import lax
from jax.experimental import pallas as pl
from jax.experimental.pallas import tpu as pltpu
from jax.sharding import PartitionSpec as P

MESH = pl.DeviceIdType.MESH
EDGE = 16


def flipped(index, distance):
    bit = 1
    while bit <= distance:
        if distance & bit:
            index = index + bit * (1 - 2 * (lax.div(index, bit) % 2))
        bit *= 2
    return index


def passed_along(block, axis, distance):
    devices = range(lax.axis_size(axis))
    route = [(i - distance, i) for i in devices if i - distance in devices]
    return lax.ppermute(block, axis, route)


def exchange_kernel(n, out_ref, in_ref, send_sem, recv_sem, own_sem):
    me = lax.axis_index("ctx")
    mp = lax.axis_index("mp")
    barrier = pltpu.get_barrier_semaphore()
    for d in range(1, n):
        pl.semaphore_signal(barrier, inc=1, device_id=(flipped(me, d), mp), device_id_type=MESH)
    pl.semaphore_wait(barrier, n - 1)
    copies = []
    for d in reversed(range(1, n)):
        peer = flipped(me, d)
        copy = pltpu.make_async_remote_copy(
            src_ref=out_ref.at[peer],
            dst_ref=in_ref.at[me],
            send_sem=send_sem.at[d],
            recv_sem=recv_sem.at[d],
            device_id=(peer, mp),
            device_id_type=MESH,
        )
        copy.start()
        copies.append(copy)
    own = pltpu.make_async_copy(out_ref.at[me], in_ref.at[me], own_sem)
    own.start()
    own.wait()
    for d in range(1, n):
        peer = flipped(me, d)
        pltpu.make_async_remote_copy(
            src_ref=out_ref.at[peer],
            dst_ref=in_ref.at[peer],
            send_sem=send_sem.at[d],
            recv_sem=recv_sem.at[d],
            device_id=(peer, mp),
            device_id_type=MESH,
        ).wait()


def exchange(outgoing):
    n = outgoing.shape[0]
    return pl.pallas_call(
        functools.partial(exchange_kernel, n),
        out_shape=jax.ShapeDtypeStruct(outgoing.shape, outgoing.dtype),
        in_specs=[pl.BlockSpec(memory_space=pl.ANY)],
        out_specs=pl.BlockSpec(memory_space=pl.ANY),
        scratch_shapes=[
            pltpu.SemaphoreType.DMA((n,)),
            pltpu.SemaphoreType.DMA((n,)),
            pltpu.SemaphoreType.DMA,
        ],
        compiler_params=pltpu.CompilerParams(collective_id=0, has_side_effects=True),
        name="exchange",
    )(outgoing)


def short_kernel(nb, wanted_ref, *refs):
    block_refs = refs[:nb]
    edge_ref, filt_ref, back_ref, q_ref, z_ref = refs[nb:]
    back = back_ref[...]
    rows, lanes = q_ref.shape
    span = filt_ref.shape[1]

    def conv(i, sl):
        ext = jnp.concatenate(
            [edge_ref[i, :, sl].astype(jnp.float32)]
            + [b[0, i, :, sl].astype(jnp.float32) for b in block_refs],
            axis=0,
        )
        total = filt_ref[i, 0:1, sl] * ext[EDGE:]
        for j in range(1, span):
            piece = ext[EDGE - j : EDGE - j + rows]
            total = total + filt_ref[i, j : j + 1, sl] * jnp.where(back >= j, piece, 0.0)
        return total

    for lo in range(0, lanes, 128):
        sl = slice(lo, lo + 128)
        q_ref[:, sl] = conv(0, sl)
        z_ref[:, sl] = (conv(1, sl) * conv(2, sl)).astype(z_ref.dtype)


def short_stage(incoming, wanted, edge, filt, back):
    n, _, blk, width = incoming.shape
    nb = wanted.shape[0]
    rows = nb * blk
    lanes = 256
    in_specs = [
        pl.BlockSpec((1, 3, blk, lanes), functools.partial(lambda k, i, w: (w[k], 0, 0, i), k))
        for k in range(nb)
    ] + [
        pl.BlockSpec((3, EDGE, lanes), lambda i, w: (0, 0, i)),
        pl.BlockSpec((3, filt.shape[1], lanes), lambda i, w: (0, 0, i)),
        pl.BlockSpec((rows, 128), lambda i, w: (0, 0)),
    ]
    return pl.pallas_call(
        functools.partial(short_kernel, nb),
        grid_spec=pltpu.PrefetchScalarGridSpec(
            num_scalar_prefetch=1,
            grid=(width // lanes,),
            in_specs=in_specs,
            out_specs=[
                pl.BlockSpec((rows, lanes), lambda i, w: (0, i)),
                pl.BlockSpec((rows, lanes), lambda i, w: (0, i)),
            ],
        ),
        out_shape=[
            jax.ShapeDtypeStruct((rows, width), jnp.float32),
            jax.ShapeDtypeStruct((rows, width), jnp.bfloat16),
        ],
        compiler_params=pltpu.CompilerParams(vmem_limit_bytes=48 * 2**20),
        name="short_conv",
    )(wanted, *([incoming] * nb), edge, filt, back)


def medium_kernel(per_group, span, prev_ref, z_ref, q_ref, skip_ref, line_ref, back_ref, h_ref):
    rows, lanes = z_ref.shape
    row = lax.broadcasted_iota(jnp.int32, (span, 2 * span), 0)
    col = lax.broadcasted_iota(jnp.int32, (span, 2 * span), 1)
    step = span + row - col
    lane = lax.broadcasted_iota(jnp.int32, (span, 128), 1)
    tiles = rows // span
    keeps = [
        step <= jnp.concatenate([back_ref[r * span : (r + 1) * span]] * 2, axis=1)
        for r in range(tiles)
    ]
    groups = 128 // per_group
    for lo in range(0, lanes, 128):
        sl = slice(lo, lo + 128)
        ext = jnp.concatenate([prev_ref[:, sl], z_ref[:, sl]], axis=0)
        total = [jnp.zeros((span, 128), jnp.float32) for _ in range(tiles)]
        for g in range(groups):
            line = line_ref[0, lo // per_group + g : lo // per_group + g + 1, :]
            band = pltpu.roll(
                jnp.broadcast_to(line, (span, 2 * span)), 0, 1, stride=1, stride_axis=0
            )
            mine = (lane >= g * per_group) & (lane < (g + 1) * per_group)
            for r in range(tiles):
                kept = jnp.where(keeps[r], band, 0.0).astype(jnp.bfloat16)
                part = jnp.dot(
                    kept,
                    ext[r * span : (r + 2) * span],
                    preferred_element_type=jnp.float32,
                )
                total[r] = jnp.where(mine, part, total[r])
        for r in range(tiles):
            rs = slice(r * span, (r + 1) * span)
            full = total[r] + skip_ref[0:1, sl] * z_ref[rs, sl].astype(jnp.float32)
            h_ref[rs, sl] = (q_ref[rs, sl] * full).astype(h_ref.dtype)


def medium_stage(z_prev, z_vals, query, skip, taps, back):
    rows, width = z_vals.shape
    span, groups = taps.shape
    per_group = width // groups
    lanes = 256
    line = jnp.concatenate(
        [
            jnp.zeros((groups, 1), jnp.float32),
            jnp.transpose(taps[::-1]).astype(jnp.float32),
            jnp.zeros((groups, span - 1), jnp.float32),
        ],
        axis=1,
    ).reshape(width // lanes, lanes // per_group, 2 * span)
    return pl.pallas_call(
        functools.partial(medium_kernel, per_group, span),
        grid=(width // lanes,),
        in_specs=[
            pl.BlockSpec((span, lanes), lambda i: (0, i)),
            pl.BlockSpec((rows, lanes), lambda i: (0, i)),
            pl.BlockSpec((rows, lanes), lambda i: (0, i)),
            pl.BlockSpec((1, lanes), lambda i: (0, i)),
            pl.BlockSpec((1, lanes // per_group, 2 * span), lambda i: (i, 0, 0)),
            pl.BlockSpec((rows, 128), lambda i: (0, 0)),
        ],
        out_specs=pl.BlockSpec((rows, lanes), lambda i: (0, i)),
        out_shape=jax.ShapeDtypeStruct((rows, width), jnp.bfloat16),
        compiler_params=pltpu.CompilerParams(vmem_limit_bytes=48 * 2**20),
        name="medium_conv",
    )(z_prev, z_vals, query, skip, line, back)


def project_kernel(
    n, m, hid_ref, w_ref, out_ref, hid, pout, near_in, far_out, far_in, keep, fin, xin,
    hsend, hrecv, nsend, nrecv, fsend, frecv, xsend, xrecv, osend, orecv,
):
    c = lax.axis_index("ctx")
    z = lax.axis_index("mp")
    share = n // m
    rows = hid_ref.shape[0]
    cols = w_ref.shape[1]
    part = rows // m
    halving = m == 4

    def part_rows(index):
        return pl.ds(pl.multiple_of(index * part, part), part)

    barrier = pltpu.get_barrier_semaphore()
    for d in range(1, n):
        pl.semaphore_signal(barrier, inc=1, device_id=(flipped(c, d), z), device_id_type=MESH)
    for s in range(1, m):
        pl.semaphore_signal(barrier, inc=1, device_id=(c, flipped(z, s)), device_id_type=MESH)
    pl.semaphore_wait(barrier, n - 1 + m - 1)

    sent = []

    def remote(src, dst, send_sem, recv_sem, device):
        return pltpu.make_async_remote_copy(
            src_ref=src,
            dst_ref=dst,
            send_sem=send_sem,
            recv_sem=recv_sem,
            device_id=device,
            device_id_type=MESH,
        )

    def send(*args):
        copy = remote(*args)
        copy.start()
        sent.append(copy)

    def send_hidden(origin, peer, slot, src):
        send(src, hid.at[origin], hsend.at[slot], hrecv.at[origin], (peer, z))

    def hidden_arrived(origin):
        remote(
            hid_ref, hid.at[origin], hsend.at[0], hrecv.at[origin], (flipped(c, 1), z)
        ).wait_recv()

    origins = []

    def multiply(origin, src):
        i = len(origins)
        origins.append(origin)

        @pl.loop(0, cols // 256)
        def _(k):
            at = pl.ds(pl.multiple_of(k * 256, 256), 256)
            pout[i, :, at] = jnp.dot(
                src[...], w_ref[:, at], preferred_element_type=jnp.float32
            ).astype(jnp.bfloat16)

        for s in [3, 1] if halving else range(1, m):
            slot = s // 2 if halving else s - 1
            peer = flipped(z, 1) if halving else flipped(z, s)
            send(
                pout.at[i, part_rows(flipped(z, s))],
                near_in.at[i, slot],
                nsend.at[i, slot],
                nrecv.at[i, slot],
                (c, peer),
            )

    mate = flipped(c, 1)
    if n == 8:
        core = c % 2
        x_peer, y_peer = flipped(c, 2), flipped(c, 4)
        first = x_peer + (y_peer - x_peer) * core
        second = y_peer + (x_peer - y_peer) * core
        across = flipped(c, 6)
        send_hidden(c, first, 1, hid_ref)
        send_hidden(c, second, 2, hid_ref)
        send_hidden(c, mate, 3, hid_ref)
        multiply(c, hid_ref)
        hidden_arrived(mate)
        multiply(mate, hid.at[mate])
        hidden_arrived(first)
        send_hidden(first, second, 4, hid.at[first])
        send_hidden(first, mate, 5, hid.at[first])
        hidden_arrived(second)
        send_hidden(second, mate, 6, hid.at[second])
        multiply(first, hid.at[first])
        multiply(second, hid.at[second])
        for origin in (flipped(second, 1), flipped(first, 1)):
            hidden_arrived(origin)
            multiply(origin, hid.at[origin])
        hidden_arrived(across)
        send_hidden(across, mate, 7, hid.at[across])
        multiply(across, hid.at[across])
        hidden_arrived(flipped(across, 1))
        multiply(flipped(across, 1), hid.at[flipped(across, 1)])
    else:
        for d in range(1, n):
            send_hidden(c, flipped(c, d), d, hid_ref)
        multiply(c, hid_ref)
        for d in range(1, n):
            origin = flipped(c, d)
            hidden_arrived(origin)
            multiply(origin, hid.at[origin])

    def near_arrived(i, slot):
        remote(
            pout.at[i, part_rows(0)],
            near_in.at[i, slot],
            nsend.at[i, slot],
            nrecv.at[i, slot],
            (c, flipped(z, 1)),
        ).wait_recv()

    def finish(i, total):
        fin[i] = total.astype(jnp.bfloat16)
        if i == 0:
            pltpu.make_async_copy(fin.at[0], xin.at[c], xrecv.at[c]).start()
        else:
            send(fin.at[i], xin.at[c], xsend.at[i], xrecv.at[c], (origins[i], z))

    if halving:
        far = flipped(z, 2)
        for i in range(n):
            near_arrived(i, 1)
            far_out[i] = (
                pout[i, part_rows(far)].astype(jnp.float32) + near_in[i, 1].astype(jnp.float32)
            ).astype(jnp.bfloat16)
            send(far_out.at[i], far_in.at[i], fsend.at[i], frecv.at[i], (c, far))
            near_arrived(i, 0)
            keep[i] = pout[i, part_rows(z)].astype(jnp.float32) + near_in[i, 0].astype(jnp.float32)
        for i in range(n):
            remote(far_out.at[i], far_in.at[i], fsend.at[i], frecv.at[i], (c, far)).wait_recv()
            finish(i, keep[i] + far_in[i].astype(jnp.float32))
    else:
        for i in range(n):
            total = pout[i, part_rows(z)].astype(jnp.float32)
            for s in range(1, m):
                near_arrived(i, s - 1)
                total = total + near_in[i, s - 1].astype(jnp.float32)
            finish(i, total)

    home = lax.div(c, share)

    def forward(plane, t, h):
        return remote(
            xin.at[plane * share + h],
            out_ref.at[part_rows(z), pl.ds(h * cols, cols)],
            osend.at[t, h],
            orecv.at[z, h],
            (c, plane),
        )

    for t in range(m):
        plane = flipped(home, t)
        for h in range(share):
            block = plane * share + h
            pltpu.make_async_copy(fin.at[0], xin.at[block], xrecv.at[block]).wait()

            @pl.when(plane != z)
            def _(plane=plane, t=t, h=h):
                forward(plane, t, h).start()

    for h in range(share):
        out_ref[part_rows(z), pl.ds(h * cols, cols)] = xin[z * share + h]
    for s in range(1, m):
        other = flipped(z, s)
        for h in range(share):
            remote(
                xin.at[0],
                out_ref.at[part_rows(other), pl.ds(h * cols, cols)],
                osend.at[0, 0],
                orecv.at[other, h],
                (c, other),
            ).wait_recv()

    for copy in sent:
        copy.wait_send()
    for t in range(m):
        plane = flipped(home, t)
        for h in range(share):

            @pl.when(plane != z)
            def _(plane=plane, t=t, h=h):
                forward(plane, t, h).wait_send()


def project(hidden, weight):
    n, m = lax.axis_size("ctx"), lax.axis_size("mp")
    share = n // m
    rows, depth = hidden.shape
    cols = weight.shape[1]
    part = rows // m
    near = 2 if m == 4 else m - 1
    bf16 = jnp.bfloat16
    dma = pltpu.SemaphoreType.DMA
    return pl.pallas_call(
        functools.partial(project_kernel, n, m),
        out_shape=jax.ShapeDtypeStruct((rows, share * cols), bf16),
        in_specs=[pl.BlockSpec(memory_space=pltpu.VMEM)] * 2,
        out_specs=pl.BlockSpec(memory_space=pltpu.VMEM),
        scratch_shapes=[
            pltpu.VMEM((n, rows, depth), bf16),
            pltpu.VMEM((n, rows, cols), bf16),
            pltpu.VMEM((n, near, part, cols), bf16),
            pltpu.VMEM((n, part, cols), bf16),
            pltpu.VMEM((n, part, cols), bf16),
            pltpu.VMEM((n, part, cols), jnp.float32),
            pltpu.VMEM((n, part, cols), bf16),
            pltpu.VMEM((n, part, cols), bf16),
            dma((n,)),
            dma((n,)),
            dma((n, near)),
            dma((n, near)),
            dma((n,)),
            dma((n,)),
            dma((n,)),
            dma((n,)),
            dma((m, share)),
            dma((m, share)),
        ],
        compiler_params=pltpu.CompilerParams(
            collective_id=1, has_side_effects=True, vmem_limit_bytes=50 * 2**20
        ),
        name="project",
    )(hidden, weight)


def on_device(
    source_rows,
    short_filters,
    medium_filters,
    skip_gain,
    out_weight,
    doc_lengths,
    block_packing_device,
):
    stretches = lax.axis_size("ctx")
    me = lax.axis_index("ctx")
    nb_own = block_packing_device.shape[1]
    blk = source_rows.shape[0] // stretches
    rows = nb_own * blk
    width = source_rows.shape[2]
    mr_len = medium_filters.shape[0]
    member = jnp.any(block_packing_device == me, axis=1)
    flags = member.astype(jnp.int32)
    slots = jnp.minimum(jnp.cumsum(flags) - flags, stretches - 1)
    blocks = source_rows.reshape(stretches, blk, 3, width)
    outgoing = jnp.take(blocks, slots, axis=0, mode="clip").transpose(0, 2, 1, 3)
    incoming = exchange(outgoing)
    wanted = lax.dynamic_index_in_dim(block_packing_device, me, 0, keepdims=False)

    ends = jnp.cumsum(doc_lengths)
    starts = ends - doc_lengths
    positions = me * rows + jnp.arange(rows, dtype=jnp.int32)
    begin = jnp.max(jnp.where(starts[None, :] <= positions[:, None], starts[None, :], 0), axis=1)
    back = jnp.broadcast_to((positions - begin)[:, None], (rows, 128))

    last = lax.dynamic_index_in_dim(incoming, wanted[nb_own - 1], 0, keepdims=False)
    edge = passed_along(last[:, blk - EDGE :], "ctx", 1)
    query, z_vals = short_stage(incoming, wanted, edge, short_filters.astype(jnp.float32), back)
    z_prev = passed_along(z_vals[rows - mr_len :], "ctx", 1)
    hidden = medium_stage(z_prev, z_vals, query, skip_gain[None, :], medium_filters, back)
    return project(hidden, out_weight)


def solution(mesh):
    return jax.shard_map(
        on_device,
        mesh=mesh,
        in_specs=(
            P("ctx", None, "mp"),
            P(None, None, "mp"),
            P(None, "mp"),
            P("mp"),
            P("mp", "ctx"),
            P(),
            P(),
        ),
        out_specs=P("ctx", "mp"),
        check_vma=False,
    )
```

```python
import functools

import jax
import jax.numpy as jnp
from jax import lax
from jax.experimental import pallas as pl
from jax.experimental.pallas import tpu as pltpu
from jax.sharding import PartitionSpec as P

MESH = pl.DeviceIdType.MESH
EDGE = 16


def flipped(index, distance):
    bit = 1
    while bit <= distance:
        if distance & bit:
            index = index + bit * (1 - 2 * (lax.div(index, bit) % 2))
        bit *= 2
    return index


def passed_along(block, axis, distance):
    devices = range(lax.axis_size(axis))
    route = [(i - distance, i) for i in devices if i - distance in devices]
    return lax.ppermute(block, axis, route)


def exchange_kernel(n, out_ref, in_ref, send_sem, recv_sem, own_sem):
    me = lax.axis_index("ctx")
    mp = lax.axis_index("mp")
    barrier = pltpu.get_barrier_semaphore()
    for d in range(1, n):
        pl.semaphore_signal(barrier, inc=1, device_id=(flipped(me, d), mp), device_id_type=MESH)
    pl.semaphore_wait(barrier, n - 1)
    copies = []
    for d in reversed(range(1, n)):
        peer = flipped(me, d)
        copy = pltpu.make_async_remote_copy(
            src_ref=out_ref.at[peer],
            dst_ref=in_ref.at[me],
            send_sem=send_sem.at[d],
            recv_sem=recv_sem.at[d],
            device_id=(peer, mp),
            device_id_type=MESH,
        )
        copy.start()
        copies.append(copy)
    own = pltpu.make_async_copy(out_ref.at[me], in_ref.at[me], own_sem)
    own.start()
    own.wait()
    for d in range(1, n):
        peer = flipped(me, d)
        pltpu.make_async_remote_copy(
            src_ref=out_ref.at[peer],
            dst_ref=in_ref.at[peer],
            send_sem=send_sem.at[d],
            recv_sem=recv_sem.at[d],
            device_id=(peer, mp),
            device_id_type=MESH,
        ).wait()


def exchange(outgoing):
    n = outgoing.shape[0]
    return pl.pallas_call(
        functools.partial(exchange_kernel, n),
        out_shape=jax.ShapeDtypeStruct(outgoing.shape, outgoing.dtype),
        in_specs=[pl.BlockSpec(memory_space=pl.ANY)],
        out_specs=pl.BlockSpec(memory_space=pl.ANY),
        scratch_shapes=[
            pltpu.SemaphoreType.DMA((n,)),
            pltpu.SemaphoreType.DMA((n,)),
            pltpu.SemaphoreType.DMA,
        ],
        compiler_params=pltpu.CompilerParams(collective_id=0, has_side_effects=True),
        name="exchange",
    )(outgoing)


def short_kernel(nb, wanted_ref, *refs):
    block_refs = refs[:nb]
    edge_ref, filt_ref, back_ref, q_ref, z_ref = refs[nb:]
    back = back_ref[...]
    rows, lanes = q_ref.shape
    span = filt_ref.shape[1]

    def conv(i, sl):
        ext = jnp.concatenate(
            [edge_ref[0, i, :, sl].astype(jnp.float32)]
            + [b[0, i, :, sl].astype(jnp.float32) for b in block_refs],
            axis=0,
        )
        total = filt_ref[i, 0:1, sl] * ext[EDGE:]
        for j in range(1, span):
            piece = ext[EDGE - j : EDGE - j + rows]
            total = total + filt_ref[i, j : j + 1, sl] * jnp.where(back >= j, piece, 0.0)
        return total

    for lo in range(0, lanes, 128):
        sl = slice(lo, lo + 128)
        q_ref[:, sl] = conv(0, sl)
        z_ref[:, sl] = (conv(1, sl) * conv(2, sl)).astype(z_ref.dtype)


def short_stage(incoming, wanted, half, edge, filt, back):
    n, _, blk, width = incoming.shape
    nb = wanted.shape[0] // 2
    first = half * nb
    rows = nb * blk
    lanes = 256

    def block_at(k):
        return pl.BlockSpec((1, 3, blk, lanes), lambda i, w: (w[first + k], 0, 0, i))

    if edge is None:
        edge = incoming
        edge_spec = pl.BlockSpec(
            (1, 3, EDGE, lanes), lambda i, w: (w[first - 1], 0, blk // EDGE - 1, i)
        )
    else:
        edge_spec = pl.BlockSpec((1, 3, EDGE, lanes), lambda i, w: (0, 0, 0, i))
    span = filt.shape[1]
    return pl.pallas_call(
        functools.partial(short_kernel, nb),
        grid_spec=pltpu.PrefetchScalarGridSpec(
            num_scalar_prefetch=1,
            grid=(width // lanes,),
            in_specs=[block_at(k) for k in range(nb)]
            + [
                edge_spec,
                pl.BlockSpec((3, span, lanes), lambda i, w: (0, 0, i)),
                pl.BlockSpec((rows, 128), lambda i, w: (half, 0)),
            ],
            out_specs=[
                pl.BlockSpec((rows, lanes), lambda i, w: (0, i)),
                pl.BlockSpec((rows, lanes), lambda i, w: (0, i)),
            ],
        ),
        out_shape=[
            jax.ShapeDtypeStruct((rows, width), jnp.float32),
            jax.ShapeDtypeStruct((rows, width), jnp.bfloat16),
        ],
        compiler_params=pltpu.CompilerParams(vmem_limit_bytes=48 * 2**20),
        cost_estimate=pl.CostEstimate(
            flops=9 * span * rows * width * 8, bytes_accessed=12 * rows * width, transcendentals=0
        ),
        name="short_conv",
    )(wanted, *([incoming] * nb), edge, filt, back)


def medium_kernel(per_group, span, prev_ref, z_ref, q_ref, skip_ref, line_ref, back_ref, *refs):
    h_ref = refs[-1]
    lanes = z_ref.shape[1]
    row = lax.broadcasted_iota(jnp.int32, (span, 2 * span), 0)
    col = lax.broadcasted_iota(jnp.int32, (span, 2 * span), 1)
    lane = lax.broadcasted_iota(jnp.int32, (span, 128), 1)
    keeps = span + row - col <= jnp.concatenate([back_ref[...]] * 2, axis=1)
    groups = 128 // per_group
    for lo in range(0, lanes, 128):
        sl = slice(lo, lo + 128)
        ext = jnp.concatenate([prev_ref[:, sl], z_ref[:, sl]], axis=0)
        total = jnp.zeros((span, 128), jnp.float32)
        for g in range(groups):
            line = line_ref[0, lo // per_group + g : lo // per_group + g + 1, :]
            band = pltpu.roll(
                jnp.broadcast_to(line, (span, 2 * span)), 0, 1, stride=1, stride_axis=0
            )
            kept = jnp.where(keeps, band, 0.0).astype(jnp.bfloat16)
            part = jnp.dot(kept, ext, preferred_element_type=jnp.float32)
            mine = (lane >= g * per_group) & (lane < (g + 1) * per_group)
            total = jnp.where(mine, part, total)
        full = total + skip_ref[0:1, sl] * z_ref[:, sl].astype(jnp.float32)
        h_ref[:, sl] = (q_ref[:, sl] * full).astype(h_ref.dtype)


def filter_lines(taps):
    span, groups = taps.shape
    return jnp.concatenate(
        [
            jnp.zeros((groups, 1), jnp.float32),
            jnp.transpose(taps[::-1]).astype(jnp.float32),
            jnp.zeros((groups, span - 1), jnp.float32),
        ],
        axis=1,
    )


def medium_stage(z_prev, z_vals, query, skip, taps, back, half, into):
    span, width = z_vals.shape
    groups = taps.shape[1]
    per_group = width // groups
    lanes = 256
    line = filter_lines(taps).reshape(width // lanes, lanes // per_group, 2 * span)
    in_specs = [
        pl.BlockSpec((span, lanes), lambda i: (0, i)),
        pl.BlockSpec((span, lanes), lambda i: (0, i)),
        pl.BlockSpec((span, lanes), lambda i: (0, i)),
        pl.BlockSpec((1, lanes), lambda i: (0, i)),
        pl.BlockSpec((1, lanes // per_group, 2 * span), lambda i: (i, 0, 0)),
        pl.BlockSpec((span, 128), lambda i: (half, 0)),
    ]
    args = [z_prev, z_vals, query, skip, line, back]
    aliases = {}
    if into is not None:
        aliases = {len(args): 0}
        args.append(into)
        in_specs.append(pl.BlockSpec(memory_space=pl.ANY))
    return pl.pallas_call(
        functools.partial(medium_kernel, per_group, span),
        grid=(width // lanes,),
        in_specs=in_specs,
        out_specs=pl.BlockSpec((span, lanes), lambda i: (half, i)),
        out_shape=jax.ShapeDtypeStruct((2 * span, width), jnp.bfloat16),
        input_output_aliases=aliases,
        compiler_params=pltpu.CompilerParams(vmem_limit_bytes=48 * 2**20),
        cost_estimate=pl.CostEstimate(
            flops=2 * groups * span * 2 * span * 256,
            bytes_accessed=10 * span * width,
            transcendentals=0,
        ),
        name="medium_conv",
    )(*args)


def project_kernel(
    n, m, hid_ref, w_ref, out_ref, hid, pout, near_in, far_out, far_in, keep, fin, xin,
    hsend, hrecv, nsend, nrecv, fsend, frecv, xsend, xrecv, osend, orecv,
):
    c = lax.axis_index("ctx")
    z = lax.axis_index("mp")
    share = n // m
    rows = hid_ref.shape[0]
    cols = w_ref.shape[1]
    part = rows // m
    halving = m == 4

    def part_rows(index):
        return pl.ds(pl.multiple_of(index * part, part), part)

    barrier = pltpu.get_barrier_semaphore()
    for d in range(1, n):
        pl.semaphore_signal(barrier, inc=1, device_id=(flipped(c, d), z), device_id_type=MESH)
    for s in range(1, m):
        pl.semaphore_signal(barrier, inc=1, device_id=(c, flipped(z, s)), device_id_type=MESH)
    pl.semaphore_wait(barrier, n - 1 + m - 1)

    sent = []

    def remote(src, dst, send_sem, recv_sem, device):
        return pltpu.make_async_remote_copy(
            src_ref=src,
            dst_ref=dst,
            send_sem=send_sem,
            recv_sem=recv_sem,
            device_id=device,
            device_id_type=MESH,
        )

    def send(*args):
        copy = remote(*args)
        copy.start()
        sent.append(copy)

    def send_hidden(origin, peer, slot, src):
        send(src, hid.at[origin], hsend.at[slot], hrecv.at[origin], (peer, z))

    def hidden_arrived(origin):
        remote(
            hid_ref, hid.at[origin], hsend.at[0], hrecv.at[origin], (flipped(c, 1), z)
        ).wait_recv()

    origins = []

    def multiply(origin, src):
        i = len(origins)
        origins.append(origin)

        @pl.loop(0, cols // 256)
        def _(k):
            at = pl.ds(pl.multiple_of(k * 256, 256), 256)
            pout[i, :, at] = jnp.dot(
                src[...], w_ref[:, at], preferred_element_type=jnp.float32
            ).astype(jnp.bfloat16)

        for s in [3, 1] if halving else range(1, m):
            slot = s // 2 if halving else s - 1
            peer = flipped(z, 1) if halving else flipped(z, s)
            send(
                pout.at[i, part_rows(flipped(z, s))],
                near_in.at[i, slot],
                nsend.at[i, slot],
                nrecv.at[i, slot],
                (c, peer),
            )

    mate = flipped(c, 1)
    if n == 8:
        core = c % 2
        x_peer, y_peer = flipped(c, 2), flipped(c, 4)
        first = x_peer + (y_peer - x_peer) * core
        second = y_peer + (x_peer - y_peer) * core
        across = flipped(c, 6)
        send_hidden(c, first, 1, hid_ref)
        send_hidden(c, second, 2, hid_ref)
        send_hidden(c, mate, 3, hid_ref)
        multiply(c, hid_ref)
        hidden_arrived(mate)
        multiply(mate, hid.at[mate])
        hidden_arrived(first)
        send_hidden(first, second, 4, hid.at[first])
        send_hidden(first, mate, 5, hid.at[first])
        hidden_arrived(second)
        send_hidden(second, mate, 6, hid.at[second])
        multiply(first, hid.at[first])
        multiply(second, hid.at[second])
        for origin in (flipped(second, 1), flipped(first, 1)):
            hidden_arrived(origin)
            multiply(origin, hid.at[origin])
        hidden_arrived(across)
        send_hidden(across, mate, 7, hid.at[across])
        multiply(across, hid.at[across])
        hidden_arrived(flipped(across, 1))
        multiply(flipped(across, 1), hid.at[flipped(across, 1)])
    else:
        for d in range(1, n):
            send_hidden(c, flipped(c, d), d, hid_ref)
        multiply(c, hid_ref)
        for d in range(1, n):
            origin = flipped(c, d)
            hidden_arrived(origin)
            multiply(origin, hid.at[origin])

    def near_arrived(i, slot):
        remote(
            pout.at[i, part_rows(0)],
            near_in.at[i, slot],
            nsend.at[i, slot],
            nrecv.at[i, slot],
            (c, flipped(z, 1)),
        ).wait_recv()

    def finish(i, total):
        fin[i] = total.astype(jnp.bfloat16)
        if i == 0:
            pltpu.make_async_copy(fin.at[0], xin.at[c], xrecv.at[c]).start()
        else:
            send(fin.at[i], xin.at[c], xsend.at[i], xrecv.at[c], (origins[i], z))

    if halving:
        far = flipped(z, 2)
        for i in range(n):
            near_arrived(i, 1)
            far_out[i] = (
                pout[i, part_rows(far)].astype(jnp.float32) + near_in[i, 1].astype(jnp.float32)
            ).astype(jnp.bfloat16)
            send(far_out.at[i], far_in.at[i], fsend.at[i], frecv.at[i], (c, far))
            near_arrived(i, 0)
            keep[i] = pout[i, part_rows(z)].astype(jnp.float32) + near_in[i, 0].astype(jnp.float32)
        for i in range(n):
            remote(far_out.at[i], far_in.at[i], fsend.at[i], frecv.at[i], (c, far)).wait_recv()
            finish(i, keep[i] + far_in[i].astype(jnp.float32))
    else:
        for i in range(n):
            total = pout[i, part_rows(z)].astype(jnp.float32)
            for s in range(1, m):
                near_arrived(i, s - 1)
                total = total + near_in[i, s - 1].astype(jnp.float32)
            finish(i, total)

    home = lax.div(c, share)

    def forward(plane, t, h):
        return remote(
            xin.at[plane * share + h],
            out_ref.at[part_rows(z), pl.ds(h * cols, cols)],
            osend.at[t, h],
            orecv.at[z, h],
            (c, plane),
        )

    for t in range(m):
        plane = flipped(home, t)
        for h in range(share):
            block = plane * share + h
            pltpu.make_async_copy(fin.at[0], xin.at[block], xrecv.at[block]).wait()

            @pl.when(plane != z)
            def _(plane=plane, t=t, h=h):
                forward(plane, t, h).start()

    for h in range(share):
        out_ref[part_rows(z), pl.ds(h * cols, cols)] = xin[z * share + h]
    for s in range(1, m):
        other = flipped(z, s)
        for h in range(share):
            remote(
                xin.at[0],
                out_ref.at[part_rows(other), pl.ds(h * cols, cols)],
                osend.at[0, 0],
                orecv.at[other, h],
                (c, other),
            ).wait_recv()

    for copy in sent:
        copy.wait_send()
    for t in range(m):
        plane = flipped(home, t)
        for h in range(share):

            @pl.when(plane != z)
            def _(plane=plane, t=t, h=h):
                forward(plane, t, h).wait_send()


def project(hidden, weight):
    n, m = lax.axis_size("ctx"), lax.axis_size("mp")
    share = n // m
    rows, depth = hidden.shape
    cols = weight.shape[1]
    part = rows // m
    near = 2 if m == 4 else m - 1
    bf16 = jnp.bfloat16
    dma = pltpu.SemaphoreType.DMA
    return pl.pallas_call(
        functools.partial(project_kernel, n, m),
        out_shape=jax.ShapeDtypeStruct((rows, share * cols), bf16),
        in_specs=[pl.BlockSpec(memory_space=pltpu.VMEM)] * 2,
        out_specs=pl.BlockSpec(memory_space=pltpu.VMEM),
        scratch_shapes=[
            pltpu.VMEM((n, rows, depth), bf16),
            pltpu.VMEM((n, rows, cols), bf16),
            pltpu.VMEM((n, near, part, cols), bf16),
            pltpu.VMEM((n, part, cols), bf16),
            pltpu.VMEM((n, part, cols), bf16),
            pltpu.VMEM((n, part, cols), jnp.float32),
            pltpu.VMEM((n, part, cols), bf16),
            pltpu.VMEM((n, part, cols), bf16),
            dma((n,)),
            dma((n,)),
            dma((n, near)),
            dma((n, near)),
            dma((n,)),
            dma((n,)),
            dma((n,)),
            dma((n,)),
            dma((m, share)),
            dma((m, share)),
        ],
        compiler_params=pltpu.CompilerParams(
            collective_id=1, has_side_effects=True, vmem_limit_bytes=50 * 2**20
        ),
        name="project",
    )(hidden, weight)


def on_device(
    source_rows,
    short_filters,
    medium_filters,
    skip_gain,
    out_weight,
    doc_lengths,
    block_packing_device,
):
    stretches = lax.axis_size("ctx")
    me = lax.axis_index("ctx")
    nb_own = block_packing_device.shape[1]
    blk = source_rows.shape[0] // stretches
    rows = nb_own * blk
    width = source_rows.shape[2]
    member = jnp.any(block_packing_device == me, axis=1)
    flags = member.astype(jnp.int32)
    slots = jnp.minimum(jnp.cumsum(flags) - flags, stretches - 1)
    blocks = source_rows.reshape(stretches, blk, 3, width)
    outgoing = jnp.take(blocks, slots, axis=0, mode="clip").transpose(0, 2, 1, 3)
    incoming = exchange(outgoing)
    wanted = lax.dynamic_index_in_dim(block_packing_device, me, 0, keepdims=False)

    ends = jnp.cumsum(doc_lengths)
    starts = ends - doc_lengths
    positions = me * rows + jnp.arange(rows, dtype=jnp.int32)
    begin = jnp.max(jnp.where(starts[None, :] <= positions[:, None], starts[None, :], 0), axis=1)
    back = jnp.broadcast_to((positions - begin)[:, None], (rows, 128))

    last = lax.dynamic_index_in_dim(incoming, wanted[nb_own - 1], 0, keepdims=True)
    edge = passed_along(last[:, :, blk - EDGE :], "ctx", 1)
    taps = short_filters.astype(jnp.float32)
    skip = skip_gain[None, :]
    q_late, z_late = short_stage(incoming, wanted, 1, None, taps, back)
    z_prev = passed_along(z_late, "ctx", 1)
    q_early, z_early = short_stage(incoming, wanted, 0, edge, taps, back)
    hidden = medium_stage(z_early, z_late, q_late, skip, medium_filters, back, 1, None)
    hidden = medium_stage(z_prev, z_early, q_early, skip, medium_filters, back, 0, hidden)
    return project(hidden, out_weight)


def solution(mesh):
    return jax.shard_map(
        on_device,
        mesh=mesh,
        in_specs=(
            P("ctx", None, "mp"),
            P(None, None, "mp"),
            P(None, "mp"),
            P("mp"),
            P("mp", "ctx"),
            P(),
            P(),
        ),
        out_specs=P("ctx", "mp"),
        check_vma=False,
    )
```
